1024 devices in a mesh: dp: 64 (over x, z_lo, core), tensor: 16 (over y, z_hi).
Axes of the slice: x: 4, y: 8, z: 16 (z_hi: 2, z_lo: 8; z = z_hi * 8 + z_lo), core: 2. Of those that a mesh axis runs over, the one named last changes fastest.
Arguments:
- inputs: bfloat16 [1280, 6144], P('dp', 'tensor'), may hold values from -6 to 6
- cotangent: bfloat16 [1280, 6144], P('dp', 'tensor'), may hold values from -6 to 6
- up_weight: bfloat16 [6144, 24576], P('tensor', 'dp'), may hold values from -0.078125 to 0.078125
- down_weight: bfloat16 [24576, 6144], P('dp', 'tensor'), may hold values from -0.078125 to 0.078125
- up_bias: float32 [24576], P('dp'), may hold values from -4 to 4
Outputs:
- input_grad: bfloat16 [1280, 6144], P('dp', 'tensor')
The draws below stay inside these ranges and needn't reach their ends.
All inputs are finite; a program needn't handle non-finite values.
Results may differ from the reference program's by a relative error of at most 0.024.
Values may be sent and summed in bfloat16 or wider, within the bound.
A program may use at most 32 MiB of HBM per device.

```python
import jax
import jax.numpy as jnp
from jax import lax

D = 6144
FF = 24576
ROWS = 1280
N_TENSOR = 16


def block_levels(rng, dims, cuts, least, largest):
    def one(dim, parts):
        heights = jax.random.uniform(jax.random.fold_in(jax.random.fold_in(rng, 6), dim), (parts,), jnp.float32, least / len(cuts), largest / len(cuts))
        return jnp.repeat(jnp.exp(heights), dims[dim] // parts).reshape((-1,) + (1,) * (len(dims) - dim - 1))

    level = one(*cuts[0])
    for cut in cuts[1:]:
        level = level * one(*cut)
    return level


def bell_draw(own_key, shape, deviation, reach, shards=(), kind=jnp.bfloat16):
    gain = block_levels(own_key, shape, shards, -0.22, 0.18) if shards else 1.0
    array = jax.random.normal(own_key, shape, jnp.float32) * deviation * gain
    return jnp.minimum(jnp.maximum(array, -reach), reach).astype(kind)


def setup_inputs(seed: int = 0) -> dict:
    seeds = jax.random.split(jax.random.key(seed), 6)
    inputs = bell_draw(seeds[0], (ROWS, D), 1.0, 6.0, ((0, 64), (1, 16)))
    cotangent = bell_draw(seeds[1], (ROWS, D), 1.0, 6.0, ((0, 64), (1, 16)))
    up_weight = bell_draw(seeds[2], (D, FF), D ** -0.5, 0.078125, ((0, 16), (1, 64)))
    down_weight = bell_draw(seeds[3], (FF, D), D ** -0.5, 0.078125, ((0, 64), (1, 16)))
    up_bias = bell_draw(seeds[4], (FF,), 1.0, 4.0, ((0, 64),), jnp.float32)
    return {"inputs": inputs, "cotangent": cotangent, "up_weight": up_weight, "down_weight": down_weight, "up_bias": up_bias}


def gelu_tanh(v):
    return jax.nn.gelu(v, approximate=True)

def reference(inputs, cotangent, up_weight, down_weight, up_bias):
    width = D // N_TENSOR
    rows = inputs.shape[0]

    def accumulate(carry, index):
        start = (index * width).astype(jnp.int32)
        feat_in = lax.dynamic_slice_in_dim(inputs, start, width, 1)
        feat_cot = lax.dynamic_slice_in_dim(cotangent, start, width, 1)
        w_up = lax.dynamic_slice_in_dim(up_weight, start, width, 0)
        w_down = lax.dynamic_slice_in_dim(down_weight, start, width, 1)
        part_pre = jnp.dot(feat_in, w_up, preferred_element_type=jnp.float32)
        part_up = lax.dot_general(feat_cot, w_down, (((1,), (1,)), ((), ())), preferred_element_type=jnp.float32)
        part_pre = lax.optimization_barrier(part_pre.astype(jnp.bfloat16)).astype(jnp.float32)
        part_up = lax.optimization_barrier(part_up.astype(jnp.bfloat16)).astype(jnp.float32)
        return ((carry[0] + part_pre, carry[1] + part_up), None)
    empty = jnp.zeros((rows, FF), jnp.float32)
    (pre_sum, upstream), _ = lax.scan(accumulate, (empty, empty), jnp.arange(N_TENSOR, dtype=jnp.int32))
    pre_act = pre_sum + up_bias[None, :]
    _, back = jax.vjp(gelu_tanh, pre_act)
    hidden_grad = back(upstream)[0].astype(jnp.bfloat16)
    input_grad = lax.dot_general(hidden_grad, up_weight, (((1,), (1,)), ((), ())), preferred_element_type=jnp.float32)
    return input_grad.astype(jnp.bfloat16)
```

```python
import functools

import jax
import jax.numpy as jnp
import numpy as np
from jax import lax
from jax.experimental import pallas as pl
from jax.experimental.pallas import tpu as pltpu
from jax.sharding import PartitionSpec as P

MESH = pl.DeviceIdType.MESH
BF16, F32 = jnp.bfloat16, jnp.float32

NX, NZ, NC, NY = 4, 8, 2, 8
OWN = 20
SLAB = 48
W = 384
CHUNKS, SLOTS = 2, 4
BLOCK = SLOTS * OWN
OUT = 32

OFFSETS = ((0, 1, 7, 2), (6, 3, 5, 4))
WHERE = {off: (k, j) for k, row in enumerate(OFFSETS) for j, off in enumerate(row)}

SQRT_2_OVER_PI = 0.7978845608028654
CUBE = 0.044715


def select_matrices():
    pack = np.zeros((2 * BLOCK, SLOTS * SLAB), np.float32)
    spread = np.zeros((SLOTS * OUT, BLOCK), np.float32)
    for j in range(SLOTS):
        for r in range(OWN):
            pack[j * OWN + r, j * SLAB + r] = 1.0
            pack[BLOCK + j * OWN + r, j * SLAB + OWN + r] = 1.0
            spread[j * OUT + r, j * OWN + r] = 1.0
    return jnp.asarray(pack, BF16), jnp.asarray(spread, BF16)


def dot(a, b):
    return jnp.dot(a, b, preferred_element_type=F32)


def dot_t(a, b):
    return lax.dot_general(a, b, (((1,), (1,)), ((), ())), preferred_element_type=F32)


def gelu_slope(v):
    u = SQRT_2_OVER_PI * (v + CUBE * (v * v * v))
    t = jnp.tanh(u)
    du = SQRT_2_OVER_PI * (1.0 + (3.0 * CUBE) * (v * v))
    return 0.5 * (1.0 + t) + 0.5 * v * (1.0 - t * t) * du


def kernel(
    slab_ref, up_ref, down_ref, bias_ref, pack_ref, spread_ref, out_ref,
    gath, part, ysend, yrecv, zsend, zrecv, hid, prod, csend, crecv, xsend, xrecv, fsend, frecv,
    az_s, az_r, ax_s, ax_r, ac_s, ac_r, y_s, y_r, zh_s, zh_r, h_s, h_r, c_s, c_r, x_s, x_r, f_s, f_r,
):
    d, t = lax.axis_index("dp"), lax.axis_index("tensor")
    x, z, c = d // (NZ * NC), (d // NC) % NZ, d % NC
    y, zh = t // 2, t % 2
    ring = jnp.where(z % 2 == 0, z // 2, NZ - 1 - z // 2)

    def dev(x=x, z=z, c=c, y=y, zh=zh):
        return ((x * NZ + z) * NC + c, y * 2 + zh)

    def at_ring(off):
        r = (ring + off) % NZ
        return dev(z=jnp.where(r < NZ // 2, 2 * r, 2 * NZ - 1 - 2 * r))

    def at_x(off):
        return dev(x=(x + off) % NX)

    def at_y(off):
        return dev(y=(y + off) % NY)

    sibling, far = dev(c=1 - c), dev(zh=1 - zh)

    sends = []

    def send(src, dst, ssem, rsem, device):
        copy = pltpu.make_async_remote_copy(
            src_ref=src, dst_ref=dst, send_sem=ssem, recv_sem=rsem, device_id=device, device_id_type=MESH
        )
        copy.start()
        sends.append(copy)

    def arrived(ref, rsem):
        pltpu.make_async_copy(ref, ref, rsem).wait()

    peers = [sibling, far, at_y(1), at_y(-1)]
    peers += [at_x(o) for o in range(1, NX)] + [at_ring(o) for o in range(1, NZ)]
    barrier = pltpu.get_barrier_semaphore()
    for peer in peers:
        pl.semaphore_signal(barrier, inc=1, device_id=peer, device_id_type=MESH)
    gath[0, 0, pl.ds(c, 1), 0:SLAB, :] = slab_ref[...][None]
    pl.semaphore_wait(barrier, len(peers))

    def zslot(off):
        k, j = WHERE[off % NZ]
        return gath.at[k, 0, c, pl.ds(SLAB * j, SLAB)]

    def z_send(off, way):
        src = slab_ref if off == 0 else zslot(off)
        at = (off - way) % NZ
        send(src, zslot(at), az_s.at[at], az_r.at[at], at_ring(way))

    def z_wait(off):
        off %= NZ
        arrived(zslot(off), az_r.at[off])

    HALF = SLOTS * SLAB // 2

    def x_send_own(k):
        for i, way in enumerate((1, -1)):
            send(gath.at[k, 0, c], gath.at[k, -way % NX, c], ax_s.at[k, i], ax_r.at[k, i], at_x(way))

    def x_pass(k, i):
        way = (1, -1)[i]
        q = -way % NX
        arrived(gath.at[k, q, c], ax_r.at[k, i])
        rows = pl.ds(HALF * i, HALF)
        send(gath.at[k, q, c, rows], gath.at[k, 2, c, rows], ax_s.at[k, 2 + i], ax_r.at[k, 2 + i], at_x(way))
        core_send(k, q)

    def x_last(k):
        for i in range(2):
            arrived(gath.at[k, 2, c, pl.ds(HALF * i, HALF)], ax_r.at[k, 2 + i])
        core_send(k, 2)

    def core_send(k, q):
        send(gath.at[k, q, c], gath.at[k, q, c], ac_s.at[k, q], ac_r.at[k, q], sibling)

    def core_wait(k):
        for q in range(NX):
            arrived(gath.at[k, q, 1 - c], ac_r.at[k, q])

    def partial(k, dist):
        o = (y + dist) % NY
        rows = dot(pack_ref[...], gath[k, o // NC, o % NC]).astype(BF16)
        part[k, dist % NY, 0] = dot(rows[:BLOCK], up_ref[...])
        part[k, dist % NY, 1] = dot_t(rows[BLOCK:], down_ref[...])

    def y_step(k, m):
        dist = 4 - (m + 1) // 2
        for i, way in enumerate((1, -1)):
            which = (m + 1 + i) % 2
            total = part[k, (way * dist) % NY, which]
            if m >= 2:
                arrived(yrecv.at[k, i, m - 2], y_r.at[k, i, m - 2])
                total = total + yrecv[k, i, m - 2].astype(F32)
            ysend[k, i, m] = total.astype(BF16)
            send(ysend.at[k, i, m], yrecv.at[k, i, m], y_s.at[k, i, m], y_r.at[k, i, m], at_y(way))

    def y_last(k):
        for i in range(2):
            arrived(yrecv.at[k, i, 5], y_r.at[k, i, 5])
            which = i
            part[k, 0, which] = part[k, 0, which] + yrecv[k, i, 5].astype(F32)
        for i in range(2):
            arrived(yrecv.at[k, i, 6], y_r.at[k, i, 6])
            which = 1 - i
            total = part[k, 0, which] + yrecv[k, i, 6].astype(F32)
            part[k, 0, which] = total
        for which in range(2):
            zsend[k, which] = part[k, 0, which].astype(BF16)
            send(zsend.at[k, which], zrecv.at[k, which], zh_s.at[k, which], zh_r.at[k, which], far)

    def hidden(k):
        arrived(zrecv.at[k, 0], zh_r.at[k, 0])
        slope = gelu_slope(part[k, 0, 0] + zrecv[k, 0].astype(F32) + bias_ref[...])
        arrived(zrecv.at[k, 1], zh_r.at[k, 1])
        value = ((part[k, 0, 1] + zrecv[k, 1].astype(F32)) * slope).astype(BF16)
        hid[k, pl.ds(y, 1)] = value[None]

    def h_piece(k, o, s, i):
        if s < 4:
            return hid.at[k, o % NY]
        return hid.at[k, o % NY, pl.ds(0, 48) if i == 0 else pl.ds(48, 32)]

    def h_send(k, s):
        for i, way in enumerate((1, -1)):
            piece = h_piece(k, y - way * (s - 1) + NY, s, i)
            send(piece, piece, h_s.at[k, i, s - 1], h_r.at[k, i, s - 1], at_y(way))

    def h_wait(k, s):
        for i, way in enumerate((1, -1)):
            arrived(h_piece(k, y - way * s + NY, s, i), h_r.at[k, i, s - 1])

    def product(k):
        @pl.loop(0, NX)
        def _(q):
            for cc in range(NC):
                prod[k, q, cc] = dot_t(hid[k, q * NC + cc], up_ref[...])

        csend[k] = prod[k, :, 1 - c].astype(BF16)
        send(csend.at[k], crecv.at[k], c_s.at[k], c_r.at[k], sibling)

    def over_cores(k):
        arrived(crecv.at[k], c_r.at[k])
        for q in (2, 1, 3, 0):
            total = prod[k, q, c] + crecv[k, q].astype(F32)
            if q == 0:
                prod[k, 0, 0] = total
            else:
                xsend[k, q - 1] = total.astype(BF16)
                send(xsend.at[k, q - 1], xrecv.at[k, q - 1], x_s.at[k, q - 1], x_r.at[k, q - 1], at_x(q))

    def over_x(k):
        total = prod[k, 0, 0]
        for q in (1, 3, 2):
            arrived(xrecv.at[k, q - 1], x_r.at[k, q - 1])
            total = total + xrecv[k, q - 1].astype(F32)
        slabs = dot(spread_ref[...], total.astype(BF16)).astype(BF16)
        fsend[k] = slabs.reshape(SLOTS, OUT, W)
        for j in range(SLOTS):
            off = OFFSETS[k][j]
            if off:
                send(fsend.at[k, j], frecv.at[k, j], f_s.at[k, j], f_r.at[k, j], at_ring(off))

    def over_z():
        total = fsend[0, 0].astype(F32)
        for k in range(CHUNKS):
            for j in range(SLOTS):
                if OFFSETS[k][j]:
                    arrived(frecv.at[k, j], f_r.at[k, j])
                    total = total + frecv[k, j].astype(F32)
        out_ref[...] = total[:OWN].astype(BF16)

    z_send(0, 1)
    z_send(0, -1)
    z_wait(-1)
    z_send(-1, 1)
    z_wait(1)
    z_send(1, -1)
    z_wait(2)
    x_send_own(0)
    z_send(2, -1)
    core_send(0, 0)
    z_wait(-2)
    z_send(-2, 1)
    x_pass(0, 0)
    x_pass(0, 1)
    z_wait(-3)
    z_send(-3, 1)
    z_wait(3)
    x_last(0)
    core_wait(0)
    partial(0, 4)
    y_step(0, 0)
    partial(0, 3)
    partial(0, -3)
    y_step(0, 1)
    z_wait(4)
    x_send_own(1)
    core_send(1, 0)
    y_step(0, 2)
    partial(0, 2)
    partial(0, -2)
    y_step(0, 3)
    y_step(0, 4)
    x_pass(1, 0)
    x_pass(1, 1)
    partial(0, 1)
    partial(0, -1)
    y_step(0, 5)
    y_step(0, 6)
    partial(0, 0)
    x_last(1)
    core_wait(1)
    partial(1, 4)
    y_step(1, 0)
    partial(1, 3)
    partial(1, -3)
    y_step(1, 1)
    y_last(0)
    y_step(1, 2)
    partial(1, 2)
    partial(1, -2)
    y_step(1, 3)
    y_step(1, 4)
    partial(1, 1)
    partial(1, -1)
    partial(1, 0)
    y_step(1, 5)
    y_step(1, 6)
    y_last(1)
    hidden(0)
    for s in range(1, 5):
        h_send(0, s)
        h_wait(0, s)
    product(0)
    hidden(1)
    h_send(1, 1)
    over_cores(0)
    h_wait(1, 1)
    h_send(1, 2)
    over_x(0)
    h_wait(1, 2)
    h_send(1, 3)
    h_wait(1, 3)
    h_send(1, 4)
    h_wait(1, 4)
    product(1)
    over_cores(1)
    over_x(1)
    over_z()
    for copy in sends:
        copy.wait_send()


def body(inputs, cotangent, up_weight, down_weight, up_bias):
    slab = jnp.concatenate([inputs, cotangent, jnp.zeros((SLAB - 2 * OWN, W), BF16)])
    pack, spread = select_matrices()
    vmem, dma = pltpu.VMEM, pltpu.SemaphoreType.DMA
    scratch = [
        vmem((CHUNKS, NX, NC, SLOTS * SLAB, W), BF16),
        vmem((CHUNKS, NY, 2, BLOCK, W), F32),
        vmem((CHUNKS, 2, 7, BLOCK, W), BF16),
        vmem((CHUNKS, 2, 7, BLOCK, W), BF16),
        vmem((CHUNKS, 2, BLOCK, W), BF16),
        vmem((CHUNKS, 2, BLOCK, W), BF16),
        vmem((CHUNKS, NY, BLOCK, W), BF16),
        vmem((CHUNKS, NX, NC, BLOCK, W), F32),
        vmem((CHUNKS, NX, BLOCK, W), BF16),
        vmem((CHUNKS, NX, BLOCK, W), BF16),
        vmem((CHUNKS, NX - 1, BLOCK, W), BF16),
        vmem((CHUNKS, NX - 1, BLOCK, W), BF16),
        vmem((CHUNKS, SLOTS, OUT, W), BF16),
        vmem((CHUNKS, SLOTS, OUT, W), BF16),
    ]
    for shape in (
        (NZ,), (CHUNKS, 4), (CHUNKS, NX), (CHUNKS, 2, 7), (CHUNKS, 2), (CHUNKS, 2, 4),
        (CHUNKS,), (CHUNKS, NX - 1), (CHUNKS, SLOTS),
    ):
        scratch += [dma(shape), dma(shape)]
    return pl.pallas_call(
        kernel,
        out_shape=jax.ShapeDtypeStruct((OWN, W), BF16),
        in_specs=[pl.BlockSpec(memory_space=pltpu.VMEM)] * 6,
        out_specs=pl.BlockSpec(memory_space=pltpu.VMEM),
        scratch_shapes=scratch,
        compiler_params=pltpu.CompilerParams(
            collective_id=0, has_side_effects=True, vmem_limit_bytes=48 << 20
        ),
        name="mlp_input_grad",
    )(slab, up_weight, down_weight, up_bias[None, :], pack, spread)


def solution(mesh):
    return jax.shard_map(
        body,
        mesh=mesh,
        in_specs=(
            P("dp", "tensor"),
            P("dp", "tensor"),
            P("tensor", "dp"),
            P("dp", "tensor"),
            P("dp"),
        ),
        out_specs=P("dp", "tensor"),
        check_vma=False,
    )
```

```python
import functools

import jax
import jax.numpy as jnp
import numpy as np
from jax import lax
from jax.experimental import pallas as pl
from jax.experimental.pallas import tpu as pltpu
from jax.sharding import PartitionSpec as P

MESH = pl.DeviceIdType.MESH
BF16, F32 = jnp.bfloat16, jnp.float32

NX, NZ, NC, NY = 4, 8, 2, 8
OWN = 20
SLAB = 48
W = 384
CHUNKS, SLOTS = 2, 4
BLOCK = SLOTS * OWN
OUT = 32

OFFSETS = ((0, 1, 7, 2), (6, 3, 5, 4))
WHERE = {off: (k, j) for k, row in enumerate(OFFSETS) for j, off in enumerate(row)}

SQRT_2_OVER_PI = 0.7978845608028654
CUBE = 0.044715


def select_matrices():
    pack = np.zeros((2 * BLOCK, SLOTS * SLAB), np.float32)
    spread = np.zeros((SLOTS * OUT, BLOCK), np.float32)
    for j in range(SLOTS):
        for r in range(OWN):
            pack[j * OWN + r, j * SLAB + r] = 1.0
            pack[BLOCK + j * OWN + r, j * SLAB + OWN + r] = 1.0
            spread[j * OUT + r, j * OWN + r] = 1.0
    return jnp.asarray(pack, BF16), jnp.asarray(spread, BF16)


def dot(a, b):
    return jnp.dot(a, b, preferred_element_type=F32)


def dot_t(a, b):
    return lax.dot_general(a, b, (((1,), (1,)), ((), ())), preferred_element_type=F32)


def gelu_slope(v):
    u = SQRT_2_OVER_PI * (v + CUBE * (v * v * v))
    t = jnp.tanh(u)
    du = SQRT_2_OVER_PI * (1.0 + (3.0 * CUBE) * (v * v))
    return 0.5 * (1.0 + t) + 0.5 * v * (1.0 - t * t) * du


def kernel(
    slab_ref, up_hbm, down_hbm, bias_hbm, pack_hbm, spread_hbm, out_ref,
    up_ref, down_ref, bias_ref, pack_ref, spread_ref,
    gath, part, ysend, yrecv, zsend, zrecv, hid, prod, csend, crecv, xsend, xrecv, fsend, frecv,
    az_s, az_r, ax_s, ax_r, ac_s, ac_r, y_s, y_r, zh_s, zh_r, h_s, h_r, c_s, c_r, x_s, x_r, f_s, f_r, load_s,
):
    d, t = lax.axis_index("dp"), lax.axis_index("tensor")
    x, z, c = d // (NZ * NC), (d // NC) % NZ, d % NC
    y, zh = t // 2, t % 2
    ring = jnp.where(z % 2 == 0, z // 2, NZ - 1 - z // 2)

    def dev(x=x, z=z, c=c, y=y, zh=zh):
        return ((x * NZ + z) * NC + c, y * 2 + zh)

    def at_ring(off):
        r = (ring + off) % NZ
        return dev(z=jnp.where(r < NZ // 2, 2 * r, 2 * NZ - 1 - 2 * r))

    def at_x(off):
        return dev(x=(x + off) % NX)

    def at_y(off):
        return dev(y=(y + off) % NY)

    sibling, far = dev(c=1 - c), dev(zh=1 - zh)

    sends = []

    def send(src, dst, ssem, rsem, device):
        copy = pltpu.make_async_remote_copy(
            src_ref=src, dst_ref=dst, send_sem=ssem, recv_sem=rsem, device_id=device, device_id_type=MESH
        )
        copy.start()
        sends.append(copy)

    def arrived(ref, rsem):
        pltpu.make_async_copy(ref, ref, rsem).wait()

    def left(src, dst, ssem, rsem, device):
        pltpu.make_async_remote_copy(
            src_ref=src, dst_ref=dst, send_sem=ssem, recv_sem=rsem, device_id=device, device_id_type=MESH
        ).wait_send()

    loads = []
    for i, (src, dst) in enumerate(
        ((up_hbm, up_ref), (down_hbm, down_ref), (bias_hbm, bias_ref), (pack_hbm, pack_ref), (spread_hbm, spread_ref))
    ):
        loads.append(pltpu.make_async_copy(src, dst, load_s.at[i]))
        loads[-1].start()

    peers = [sibling, far, at_y(1), at_y(-1)]
    peers += [at_x(o) for o in range(1, NX)] + [at_ring(o) for o in range(1, NZ)]
    barrier = pltpu.get_barrier_semaphore()
    for peer in peers:
        pl.semaphore_signal(barrier, inc=1, device_id=peer, device_id_type=MESH)
    gath[0, 0, pl.ds(c, 1), 0:SLAB, :] = slab_ref[...][None]
    pl.semaphore_wait(barrier, len(peers))

    def slot(off, q=0, rows=SLAB, start=0):
        k, j = WHERE[off % NZ]
        return gath.at[k, q % NX, c, pl.ds(SLAB * j + start, rows)]

    def z_own():
        for way in (2, -2, 1, -1):
            at = -way % NZ
            send(slab_ref, slot(at), az_s.at[at], az_r.at[at], at_ring(way))
        x_send(0)

    def z_pass(way):
        off = -2 * way % NZ
        arrived(slot(off), az_r.at[off])
        at = -3 * way % NZ
        send(slot(off), slot(at), az_s.at[at], az_r.at[at], at_ring(way))
        rows, start, i = (32, 0, 4) if way == 1 else (16, 32, 0)
        send(slot(off, 0, rows, start), slot(4, 0, rows, start), az_s.at[i], az_r.at[i], at_ring(2 * way))
        x_send(off)

    def z_take(off):
        off %= NZ
        if off == 4:
            arrived(slot(4, 0, 32, 0), az_r.at[4])
            arrived(slot(4, 0, 16, 32), az_r.at[0])
        else:
            arrived(slot(off), az_r.at[off])
        x_send(off)

    def x_send(off):
        for i, way in enumerate((1, -1)):
            src = slab_ref if off == 0 else slot(off)
            send(src, slot(off, -way), ax_s.at[i, off], ax_r.at[i, off], at_x(way))

    def x_take(off):
        off %= NZ
        for i, way in enumerate((1, -1)):
            arrived(slot(off, -way), ax_r.at[i, off])
            if i == WHERE[off][1] % 2:
                send(slot(off, -way), slot(off, 2), ax_s.at[2, off], ax_r.at[2, off], at_x(way))

    def x_last(k):
        for off in OFFSETS[k]:
            arrived(slot(off, 2), ax_r.at[2, off])
        core_send(k, 2)

    def core_send(k, q):
        send(gath.at[k, q, c], gath.at[k, q, c], ac_s.at[k, q], ac_r.at[k, q], sibling)

    def core_wait(k):
        for q in range(NX):
            arrived(gath.at[k, q, 1 - c], ac_r.at[k, q])

    def partial(k, dist):
        o = (y + dist) % NY
        rows = dot(pack_ref[...], gath[k, o // NC, o % NC]).astype(BF16)
        part[k, dist % NY, 0] = dot(rows[:BLOCK], up_ref[...])
        part[k, dist % NY, 1] = dot_t(rows[BLOCK:], down_ref[...])

    def y_step(k, m):
        dist = 4 - (m + 1) // 2
        for i, way in enumerate((1, -1)):
            which = (m + 1 + i) % 2
            total = part[k, (way * dist) % NY, which]
            if m >= 2:
                arrived(yrecv.at[k, i, m - 2], y_r.at[k, i, m - 2])
                total = total + yrecv[k, i, m - 2].astype(F32)
            ysend[k, i, m] = total.astype(BF16)
            send(ysend.at[k, i, m], yrecv.at[k, i, m], y_s.at[k, i, m], y_r.at[k, i, m], at_y(way))

    def y_last(k):
        for i in range(2):
            arrived(yrecv.at[k, i, 5], y_r.at[k, i, 5])
            which = i
            part[k, 0, which] = part[k, 0, which] + yrecv[k, i, 5].astype(F32)
        for i in range(2):
            arrived(yrecv.at[k, i, 6], y_r.at[k, i, 6])
            which = 1 - i
            total = part[k, 0, which] + yrecv[k, i, 6].astype(F32)
            part[k, 0, which] = total
        for which in range(2):
            zsend[k, which] = part[k, 0, which].astype(BF16)
            send(zsend.at[k, which], zrecv.at[k, which], zh_s.at[k, which], zh_r.at[k, which], far)

    def hidden(k):
        arrived(zrecv.at[k, 0], zh_r.at[k, 0])
        slope = gelu_slope(part[k, 0, 0] + zrecv[k, 0].astype(F32) + bias_ref[...])
        arrived(zrecv.at[k, 1], zh_r.at[k, 1])
        value = ((part[k, 0, 1] + zrecv[k, 1].astype(F32)) * slope).astype(BF16)
        hid[k, pl.ds(y, 1)] = value[None]

    def h_block(k, dist, rows=BLOCK, start=0):
        return hid.at[k, (y + dist + NY) % NY, pl.ds(start, rows)]

    def h_copy(k, dist, way, i, rows=BLOCK, start=0):
        piece = h_block(k, dist, rows, start)
        send(piece, piece, h_s.at[k, i], h_r.at[k, i], at_y(way))

    def h_own(k):
        for i, way in enumerate((2, -2, 1, -1)):
            h_copy(k, 0, way, i)

    def h_pass(k):
        for i, way in enumerate((1, -1)):
            arrived(h_block(k, -2 * way), h_r.at[k, i])
            h_copy(k, -2 * way, way, 4 + i)
            h_copy(k, -2 * way, 2 * way, 6 + i, *((48, 0) if way == 1 else (32, 48)))
        for i, way in enumerate((1, -1)):
            arrived(h_block(k, -way), h_r.at[k, 2 + i])

    def h_last(k):
        for i, way in enumerate((1, -1)):
            arrived(h_block(k, -3 * way), h_r.at[k, 4 + i])
            arrived(h_block(k, 4, *((48, 0) if way == 1 else (32, 48))), h_r.at[k, 6 + i])

    def pair(dist, own):
        first = y + dist + NY
        o = (first + (first + c + (0 if own else 1)) % 2) % NY
        return o // NC, o

    def product(k, dist):
        q, o = pair(dist, False)
        csend[k, q] = dot_t(hid[k, o], up_ref[...]).astype(BF16)
        copy = pltpu.make_async_remote_copy(
            src_ref=csend.at[k, q], dst_ref=crecv.at[k, q], send_sem=c_s.at[k, q], recv_sem=c_r.at[k, q],
            device_id=sibling, device_id_type=MESH,
        )
        copy.start()
        q, o = pair(dist, True)
        prod[k, q] = dot_t(hid[k, o], up_ref[...])

    def over_cores(k, dist):
        q, _ = pair(dist, True)
        arrived(crecv.at[k, q], c_r.at[k, q])
        total = prod[k, q] + crecv[k, q].astype(F32)
        prod[k, q] = total
        xsend[k, q] = total.astype(BF16)

        @pl.when(q != 0)
        def _():
            pltpu.make_async_remote_copy(
                src_ref=xsend.at[k, q], dst_ref=xrecv.at[k, q], send_sem=x_s.at[k, q], recv_sem=x_r.at[k, q],
                device_id=at_x(q), device_id_type=MESH,
            ).start()

    def over_x(k):
        total = prod[k, 0]
        for q in (1, 3, 2):
            arrived(xrecv.at[k, q], x_r.at[k, q])
            total = total + xrecv[k, q].astype(F32)
        slabs = dot(spread_ref[...], total.astype(BF16)).astype(BF16)
        fsend[k] = slabs.reshape(SLOTS, OUT, W)
        for j in range(SLOTS):
            off = OFFSETS[k][j]
            if off:
                send(fsend.at[k, j], frecv.at[k, j], f_s.at[k, j], f_r.at[k, j], at_ring(off))

    def over_z():
        total = fsend[0, 0].astype(F32)
        for k in range(CHUNKS):
            for j in range(SLOTS):
                if OFFSETS[k][j]:
                    arrived(frecv.at[k, j], f_r.at[k, j])
                    total = total + frecv[k, j].astype(F32)
        out_ref[...] = total[:OWN].astype(BF16)

    z_own()
    x_take(0)
    z_pass(1)
    z_pass(-1)
    z_take(1)
    z_take(-1)
    core_send(0, 0)
    x_take(2)
    x_take(-2)
    x_take(1)
    x_take(-1)
    core_send(0, 1)
    core_send(0, 3)
    z_take(3)
    z_take(-3)
    z_take(4)
    core_send(1, 0)
    x_last(0)
    for load in loads:
        load.wait()
    core_wait(0)
    partial(0, 4)
    y_step(0, 0)
    partial(0, 3)
    partial(0, -3)
    y_step(0, 1)
    x_take(3)
    x_take(-3)
    x_take(4)
    core_send(1, 1)
    core_send(1, 3)
    partial(0, 2)
    partial(0, -2)
    y_step(0, 2)
    y_step(0, 3)
    x_last(1)
    partial(0, 1)
    partial(0, -1)
    partial(0, 0)
    core_wait(1)
    partial(1, 4)
    y_step(1, 0)
    partial(1, 3)
    partial(1, -3)
    y_step(1, 1)
    y_step(0, 4)
    y_step(0, 5)
    partial(1, 2)
    partial(1, -2)
    y_step(1, 2)
    y_step(1, 3)
    y_step(0, 6)
    partial(1, 1)
    partial(1, -1)
    partial(1, 0)
    y_step(1, 4)
    y_step(1, 5)
    y_last(0)
    y_step(1, 6)
    y_last(1)
    hidden(0)
    h_own(0)
    h_pass(0)
    product(0, 0)
    product(0, -2)
    hidden(1)
    h_own(1)
    over_cores(0, 0)
    over_cores(0, -2)
    h_last(0)
    product(0, 2)
    product(0, 4)
    over_cores(0, 2)
    over_cores(0, 4)
    h_pass(1)
    product(1, 0)
    product(1, -2)
    over_cores(1, 0)
    over_cores(1, -2)
    over_x(0)
    h_last(1)
    product(1, 2)
    product(1, 4)
    over_cores(1, 2)
    over_cores(1, 4)
    over_x(1)
    over_z()
    for copy in sends:
        copy.wait_send()
    for k in range(CHUNKS):
        for q in range(NX):
            left(csend.at[k, q], crecv.at[k, q], c_s.at[k, q], c_r.at[k, q], sibling)
            if q:
                left(xsend.at[k, q], xrecv.at[k, q], x_s.at[k, q], x_r.at[k, q], at_x(q))


def body(inputs, cotangent, up_weight, down_weight, up_bias):
    slab = jnp.concatenate([inputs, cotangent, jnp.zeros((SLAB - 2 * OWN, W), BF16)])
    pack, spread = select_matrices()
    vmem, dma = pltpu.VMEM, pltpu.SemaphoreType.DMA
    scratch = [
        vmem((W, W), BF16),
        vmem((W, W), BF16),
        vmem((1, W), F32),
        vmem(pack.shape, BF16),
        vmem(spread.shape, BF16),
        vmem((CHUNKS, NX, NC, SLOTS * SLAB, W), BF16),
        vmem((CHUNKS, NY, 2, BLOCK, W), F32),
        vmem((CHUNKS, 2, 7, BLOCK, W), BF16),
        vmem((CHUNKS, 2, 7, BLOCK, W), BF16),
        vmem((CHUNKS, 2, BLOCK, W), BF16),
        vmem((CHUNKS, 2, BLOCK, W), BF16),
        vmem((CHUNKS, NY, BLOCK, W), BF16),
        vmem((CHUNKS, NX, BLOCK, W), F32),
        vmem((CHUNKS, NX, BLOCK, W), BF16),
        vmem((CHUNKS, NX, BLOCK, W), BF16),
        vmem((CHUNKS, NX, BLOCK, W), BF16),
        vmem((CHUNKS, NX, BLOCK, W), BF16),
        vmem((CHUNKS, SLOTS, OUT, W), BF16),
        vmem((CHUNKS, SLOTS, OUT, W), BF16),
    ]
    for shape in (
        (NZ,), (3, NZ), (CHUNKS, NX), (CHUNKS, 2, 7), (CHUNKS, 2), (CHUNKS, 8),
        (CHUNKS, NX), (CHUNKS, NX), (CHUNKS, SLOTS),
    ):
        scratch += [dma(shape), dma(shape)]
    scratch.append(dma((5,)))
    return pl.pallas_call(
        kernel,
        out_shape=jax.ShapeDtypeStruct((OWN, W), BF16),
        in_specs=[pl.BlockSpec(memory_space=pltpu.VMEM)] + [pl.BlockSpec(memory_space=pl.ANY)] * 5,
        out_specs=pl.BlockSpec(memory_space=pltpu.VMEM),
        scratch_shapes=scratch,
        compiler_params=pltpu.CompilerParams(
            collective_id=0, has_side_effects=True, vmem_limit_bytes=48 << 20
        ),
        name="mlp_input_grad",
    )(slab, up_weight, down_weight, up_bias[None, :], pack, spread)


def solution(mesh):
    return jax.shard_map(
        body,
        mesh=mesh,
        in_specs=(
            P("dp", "tensor"),
            P("dp", "tensor"),
            P("tensor", "dp"),
            P("dp", "tensor"),
            P("dp"),
        ),
        out_specs=P("dp", "tensor"),
        check_vma=False,
    )
```

```python
import functools

import jax
import jax.numpy as jnp
from jax import lax
from jax.experimental import pallas as pl
from jax.experimental.pallas import tpu as pltpu
from jax.sharding import PartitionSpec as P

MESH = pl.DeviceIdType.MESH
BF16, F32 = jnp.bfloat16, jnp.float32

NX, NZ, NC, NY = 4, 8, 2, 8
OWN = 20
W = 384
TILE = 16
WIDE = W + 128
SLAB = 2 * TILE
CHUNKS, SLOTS = 2, 4
BLOCK = SLOTS * OWN

OFFSETS = ((0, 1, 7, 2), (6, 3, 5, 4))
WHERE = {off: (k, j) for k, row in enumerate(OFFSETS) for j, off in enumerate(row)}

PARTS = ((0, 0, 48), (0, 48, 32), (1, 0, 48), (1, 48, 32))

SQRT_2_OVER_PI = 0.7978845608028654
CUBE = 0.044715


def grid_of(rows, columns):
    shape = (rows, columns)
    return lax.broadcasted_iota(jnp.int32, shape, 0), lax.broadcasted_iota(jnp.int32, shape, 1)


def ones_where(mask):
    return jnp.where(mask, 1.0, 0.0).astype(BF16)


def tail_select(group, row, column):
    return (row >= 4 * group) & (row < 4 * group + 4) & (column == TILE + row - 4 * group)


def pack_own(ref):
    i, j = grid_of(TILE, OWN)
    tail = jnp.zeros((TILE, 128), F32)
    for g in range(3):
        tail += dot(ones_where(tail_select(g, i, j)), ref[:, 128 * g : 128 * g + 128])
    return ref[0:TILE, :], tail.astype(BF16)


def unpack_select():
    i, s = grid_of(2 * BLOCK, SLOTS * SLAB)
    kind = (i >= BLOCK).astype(jnp.int32)
    r = i - BLOCK * kind
    slot = sum((r >= OWN * j).astype(jnp.int32) for j in range(1, SLOTS))
    r = r - OWN * slot
    at = SLAB * slot + TILE * kind
    yield ones_where((r < TILE) & (s == at + r))
    for g in range(3):
        yield ones_where((r >= TILE) & (s == at + 4 * g + r - TILE))


def spread_select():
    o, i = grid_of(SLOTS * TILE, BLOCK)
    slot = sum((o >= TILE * j).astype(jnp.int32) for j in range(1, SLOTS))
    r, i = o - TILE * slot, i - OWN * slot
    yield ones_where(i == r)
    for g in range(3):
        yield ones_where(tail_select(g, r, i))


def unpack_out(packed):
    r, s = grid_of(OWN, TILE)
    main = dot(ones_where((r < TILE) & (s == r)), packed[:, :W])
    tails = [dot(ones_where((r >= TILE) & (s == 4 * g + r - TILE)), packed[:, W:]) for g in range(3)]
    return main + jnp.concatenate(tails, axis=1)


def dot(a, b):
    return jnp.dot(a, b, preferred_element_type=F32)


def dot_t(a, b):
    return lax.dot_general(a, b, (((1,), (1,)), ((), ())), preferred_element_type=F32)


def gelu_slope(v):
    u = SQRT_2_OVER_PI * (v + CUBE * (v * v * v))
    t = jnp.tanh(u)
    du = SQRT_2_OVER_PI * (1.0 + (3.0 * CUBE) * (v * v))
    return 0.5 * (1.0 + t) + 0.5 * v * (1.0 - t * t) * du


def kernel(
    x_ref, cot_ref, up_hbm, down_hbm, bias_hbm, out_ref,
    up_ref, down_ref, bias_ref, slab_ref, pack_ref, spread_ref,
    gath, part, ysend, yrecv, zsend, zrecv, hid, prod, csend, crecv, xsend, xrecv, fsend, frecv,
    az_s, az_r, ax_s, ax_r, ac_s, ac_r, y_s, y_r, zh_s, zh_r, h_s, h_r, c_s, c_r, x_s, x_r, f_s, f_r, load_s,
):
    d, t = lax.axis_index("dp"), lax.axis_index("tensor")
    x, z, c = d // (NZ * NC), (d // NC) % NZ, d % NC
    y, zh = t // 2, t % 2
    ring = jnp.where(z % 2 == 0, z // 2, NZ - 1 - z // 2)

    def dev(x=x, z=z, c=c, y=y, zh=zh):
        return ((x * NZ + z) * NC + c, y * 2 + zh)

    def at_ring(off):
        r = (ring + off) % NZ
        return dev(z=jnp.where(r < NZ // 2, 2 * r, 2 * NZ - 1 - 2 * r))

    def at_x(off):
        return dev(x=(x + off) % NX)

    def at_y(off):
        return dev(y=(y + off) % NY)

    sibling, far = dev(c=1 - c), dev(zh=1 - zh)

    sends = []

    def send(src, dst, ssem, rsem, device, keep=True):
        copy = pltpu.make_async_remote_copy(
            src_ref=src, dst_ref=dst, send_sem=ssem, recv_sem=rsem, device_id=device, device_id_type=MESH
        )
        copy.start()
        if keep:
            sends.append(copy)

    def arrived(ref, rsem):
        pltpu.make_async_copy(ref, ref, rsem).wait()

    def left(src, dst, ssem, rsem, device):
        pltpu.make_async_remote_copy(
            src_ref=src, dst_ref=dst, send_sem=ssem, recv_sem=rsem, device_id=device, device_id_type=MESH
        ).wait_send()

    loads = []
    for i, (src, dst) in enumerate(
        ((up_hbm, up_ref), (down_hbm, down_ref), (bias_hbm, bias_ref))
    ):
        loads.append(pltpu.make_async_copy(src, dst, load_s.at[i]))
        loads[-1].start()

    peers = [sibling, far, at_y(1), at_y(-1)]
    peers += [at_x(o) for o in range(1, NX)] + [at_ring(o) for o in range(1, NZ)]
    barrier = pltpu.get_barrier_semaphore()
    for peer in peers:
        pl.semaphore_signal(barrier, inc=1, device_id=peer, device_id_type=MESH)
    for i, ref in enumerate((x_ref, cot_ref)):
        rows = slice(TILE * i, TILE * i + TILE)
        slab_ref[rows, :W], slab_ref[rows, W:] = pack_own(ref)
    gath[0, 0, pl.ds(c, 1), 0:SLAB, :] = slab_ref[...][None]
    pl.semaphore_wait(barrier, len(peers))

    def slot(off, q=0, rows=SLAB, start=0):
        k, j = WHERE[off % NZ]
        return gath.at[k, q % NX, c, pl.ds(SLAB * j + start, rows)]

    def z_own():
        for way in (2, -2, 1, -1):
            at = -way % NZ
            send(slab_ref, slot(at), az_s.at[at], az_r.at[at], at_ring(way))
        x_send(0)

    def z_pass(way):
        off = -2 * way % NZ
        arrived(slot(off), az_r.at[off])
        at = -3 * way % NZ
        send(slot(off), slot(at), az_s.at[at], az_r.at[at], at_ring(way))
        rows, start, i = (TILE, 0, 4) if way == 1 else (TILE, TILE, 0)
        send(slot(off, 0, rows, start), slot(4, 0, rows, start), az_s.at[i], az_r.at[i], at_ring(2 * way))
        x_send(off)

    def z_take(off):
        off %= NZ
        if off == 4:
            arrived(slot(4, 0, TILE, 0), az_r.at[4])
            arrived(slot(4, 0, TILE, TILE), az_r.at[0])
        else:
            arrived(slot(off), az_r.at[off])
        x_send(off)

    def x_send(off):
        for i, way in enumerate((1, -1)):
            src = slab_ref if off == 0 else slot(off)
            send(src, slot(off, -way), ax_s.at[i, off], ax_r.at[i, off], at_x(way))

    def x_take(off):
        off %= NZ
        for i, way in enumerate((1, -1)):
            arrived(slot(off, -way), ax_r.at[i, off])
            if i == WHERE[off][1] % 2:
                send(slot(off, -way), slot(off, 2), ax_s.at[2, off], ax_r.at[2, off], at_x(way))

    def x_last(k):
        for off in OFFSETS[k]:
            arrived(slot(off, 2), ax_r.at[2, off])
        core_send(k, 2)

    def core_send(k, q):
        send(gath.at[k, q, c], gath.at[k, q, c], ac_s.at[k, q], ac_r.at[k, q], sibling)

    def core_wait(k):
        for q in range(NX):
            arrived(gath.at[k, q, 1 - c], ac_r.at[k, q])

    def selects():
        for i, m in enumerate(unpack_select()):
            pack_ref[i] = m
        for i, m in enumerate(spread_select()):
            spread_ref[i] = m

    def partial(k, dist):
        o = (y + dist) % NY
        slabs = gath[k, o // NC, o % NC]
        tails = [dot(pack_ref[1 + g], slabs[:, W:]) for g in range(3)]
        rows = (dot(pack_ref[0], slabs[:, :W]) + jnp.concatenate(tails, axis=1)).astype(BF16)
        part[k, dist % NY, 0] = dot(rows[:BLOCK], up_ref[...])
        part[k, dist % NY, 1] = dot_t(rows[BLOCK:], down_ref[...])

    def rows_of(p):
        k, start, rows = PARTS[p]
        return k, pl.ds(start, rows)

    def y_step(p, m):
        k, rows = rows_of(p)
        dist = 4 - (m + 1) // 2
        for i, way in enumerate((1, -1)):
            which = (m + 1 + i) % 2
            total = part[k, (way * dist) % NY, which, rows, :]
            if m >= 2:
                arrived(yrecv.at[k, i, m - 2, rows], y_r.at[p, i, m - 2])
                total = total + yrecv[k, i, m - 2, rows, :].astype(F32)
            ysend[k, i, m, rows, :] = total.astype(BF16)
            send(ysend.at[k, i, m, rows], yrecv.at[k, i, m, rows], y_s.at[p, i, m], y_r.at[p, i, m], at_y(way))

    def y_last(p):
        k, rows = rows_of(p)
        for which in range(2):
            total = part[k, 0, which, rows, :]
            for i, m in ((0, 5 + which), (1, 6 - which)):
                arrived(yrecv.at[k, i, m, rows], y_r.at[p, i, m])
                total = total + yrecv[k, i, m, rows, :].astype(F32)
            part[k, 0, which, rows, :] = total
            zsend[k, which, rows, :] = total.astype(BF16)
            send(zsend.at[k, which, rows], zrecv.at[k, which, rows], zh_s.at[p, which], zh_r.at[p, which], far)

    def hidden(p):
        k, rows = rows_of(p)
        arrived(zrecv.at[k, 0, rows], zh_r.at[p, 0])
        slope = gelu_slope(part[k, 0, 0, rows, :] + zrecv[k, 0, rows, :].astype(F32) + bias_ref[...])
        arrived(zrecv.at[k, 1, rows], zh_r.at[p, 1])
        value = ((part[k, 0, 1, rows, :] + zrecv[k, 1, rows, :].astype(F32)) * slope).astype(BF16)
        hid[k, pl.ds(y, 1), rows, :] = value[None]

    def h_block(p, dist, side=None):
        k, start, rows = PARTS[p]
        if side is not None:
            first = 32 if rows == 48 else 16
            start, rows = (start, first) if side == 0 else (start + first, rows - first)
        return hid.at[k, (y + dist + NY) % NY, pl.ds(start, rows)]

    def h_copy(p, dist, way, i, side=None):
        piece = h_block(p, dist, side)
        send(piece, piece, h_s.at[p, i], h_r.at[p, i], at_y(way))

    def h_own(p):
        for i, way in enumerate((2, -2, 1, -1)):
            h_copy(p, 0, way, i)

    def h_pass(p):
        for i, way in enumerate((1, -1)):
            arrived(h_block(p, -2 * way), h_r.at[p, i])
            h_copy(p, -2 * way, way, 4 + i)
            h_copy(p, -2 * way, 2 * way, 6 + i, i)

    def h_near(p):
        for i, way in enumerate((1, -1)):
            arrived(h_block(p, -way), h_r.at[p, 2 + i])

    def h_last(p):
        for i, way in enumerate((1, -1)):
            arrived(h_block(p, -3 * way), h_r.at[p, 4 + i])
            arrived(h_block(p, 4, i), h_r.at[p, 6 + i])

    def pair(dist, own):
        first = y + dist + NY
        o = (first + (first + c + (0 if own else 1)) % 2) % NY
        return o // NC, o

    def product(k, dist):
        q, o = pair(dist, False)
        csend[k, q] = dot_t(hid[k, o], up_ref[...]).astype(BF16)
        send(csend.at[k, q], crecv.at[k, q], c_s.at[k, q], c_r.at[k, q], sibling, False)
        q, o = pair(dist, True)
        prod[k, q] = dot_t(hid[k, o], up_ref[...])

    def over_cores(k, dist):
        q, _ = pair(dist, True)
        arrived(crecv.at[k, q], c_r.at[k, q])
        total = prod[k, q] + crecv[k, q].astype(F32)
        prod[k, q] = total
        xsend[k, q] = total.astype(BF16)

        @pl.when(q != 0)
        def _():
            send(xsend.at[k, q], xrecv.at[k, q], x_s.at[k, q], x_r.at[k, q], at_x(q), False)

    def over_x(k):
        total = prod[k, 0]
        for q in (1, 3, 2):
            arrived(xrecv.at[k, q], x_r.at[k, q])
            total = total + xrecv[k, q].astype(F32)
        total = total.astype(BF16)
        fsend[k, :, :W] = dot(spread_ref[0], total).astype(BF16)
        tails = [dot(spread_ref[1 + g], total[:, 128 * g : 128 * g + 128]) for g in range(3)]
        fsend[k, :, W:] = (tails[0] + tails[1] + tails[2]).astype(BF16)
        for j in range(SLOTS):
            off, rows = OFFSETS[k][j], pl.ds(TILE * j, TILE)
            if off:
                send(fsend.at[k, rows], frecv.at[k, rows], f_s.at[k, j], f_r.at[k, j], at_ring(off))

    def over_z():
        total = fsend[0, 0:TILE, :].astype(F32)
        for k in range(CHUNKS):
            for j in range(SLOTS):
                rows = pl.ds(TILE * j, TILE)
                if OFFSETS[k][j]:
                    arrived(frecv.at[k, rows], f_r.at[k, j])
                    total = total + frecv[k, rows, :].astype(F32)
        out_ref[...] = unpack_out(total.astype(BF16)).astype(BF16)

    z_own()
    selects()
    x_take(0)
    z_pass(1)
    z_pass(-1)
    z_take(1)
    z_take(-1)
    core_send(0, 0)
    x_take(2)
    x_take(-2)
    x_take(1)
    x_take(-1)
    core_send(0, 1)
    core_send(0, 3)
    z_take(3)
    z_take(-3)
    z_take(4)
    core_send(1, 0)
    x_last(0)
    for load in loads:
        load.wait()
    core_wait(0)
    partial(0, 4)
    y_step(0, 0)
    y_step(1, 0)
    partial(0, 3)
    partial(0, -3)
    y_step(0, 1)
    y_step(1, 1)
    x_take(3)
    x_take(-3)
    x_take(4)
    core_send(1, 1)
    core_send(1, 3)
    partial(0, 2)
    partial(0, -2)
    y_step(0, 2)
    y_step(0, 3)
    y_step(1, 2)
    y_step(1, 3)
    x_last(1)
    partial(0, 1)
    partial(0, -1)
    partial(0, 0)
    core_wait(1)
    partial(1, 4)
    y_step(2, 0)
    y_step(3, 0)
    partial(1, 3)
    partial(1, -3)
    y_step(2, 1)
    y_step(0, 4)
    y_step(0, 5)
    y_step(1, 4)
    y_step(1, 5)
    y_step(3, 1)
    partial(1, 2)
    partial(1, -2)
    y_step(0, 6)
    y_last(0)
    y_step(2, 2)
    y_step(2, 3)
    y_step(1, 6)
    y_last(1)
    y_step(3, 2)
    y_step(3, 3)
    partial(1, 1)
    partial(1, -1)
    partial(1, 0)
    y_step(2, 4)
    y_step(2, 5)
    y_step(3, 4)
    y_step(3, 5)
    y_step(2, 6)
    y_last(2)
    y_step(3, 6)
    y_last(3)
    hidden(0)
    h_own(0)
    hidden(1)
    h_own(1)
    h_pass(0)
    h_pass(1)
    h_near(0)
    h_near(1)
    product(0, 0)
    product(0, -2)
    hidden(2)
    h_own(2)
    over_cores(0, 0)
    over_cores(0, -2)
    h_last(0)
    h_last(1)
    product(0, 2)
    hidden(3)
    h_own(3)
    product(0, 4)
    over_cores(0, 2)
    over_cores(0, 4)
    h_pass(2)
    h_pass(3)
    over_x(0)
    h_near(2)
    h_near(3)
    product(1, 0)
    product(1, -2)
    over_cores(1, 0)
    over_cores(1, -2)
    h_last(2)
    h_last(3)
    product(1, 2)
    product(1, 4)
    over_cores(1, 2)
    over_cores(1, 4)
    over_x(1)
    over_z()
    for copy in sends:
        copy.wait_send()
    for k in range(CHUNKS):
        for q in range(NX):
            left(csend.at[k, q], crecv.at[k, q], c_s.at[k, q], c_r.at[k, q], sibling)
            if q:
                left(xsend.at[k, q], xrecv.at[k, q], x_s.at[k, q], x_r.at[k, q], at_x(q))


def body(inputs, cotangent, up_weight, down_weight, up_bias):
    vmem, dma = pltpu.VMEM, pltpu.SemaphoreType.DMA
    scratch = [
        vmem((W, W), BF16),
        vmem((W, W), BF16),
        vmem((1, W), F32),
        vmem((SLAB, WIDE), BF16),
        vmem((4, 2 * BLOCK, SLOTS * SLAB), BF16),
        vmem((4, SLOTS * TILE, BLOCK), BF16),
        vmem((CHUNKS, NX, NC, SLOTS * SLAB, WIDE), BF16),
        vmem((CHUNKS, NY, 2, BLOCK, W), F32),
        vmem((CHUNKS, 2, 7, BLOCK, W), BF16),
        vmem((CHUNKS, 2, 7, BLOCK, W), BF16),
        vmem((CHUNKS, 2, BLOCK, W), BF16),
        vmem((CHUNKS, 2, BLOCK, W), BF16),
        vmem((CHUNKS, NY, BLOCK, W), BF16),
        vmem((CHUNKS, NX, BLOCK, W), F32),
        vmem((CHUNKS, NX, BLOCK, W), BF16),
        vmem((CHUNKS, NX, BLOCK, W), BF16),
        vmem((CHUNKS, NX, BLOCK, W), BF16),
        vmem((CHUNKS, NX, BLOCK, W), BF16),
        vmem((CHUNKS, SLOTS * TILE, WIDE), BF16),
        vmem((CHUNKS, SLOTS * TILE, WIDE), BF16),
    ]
    for shape in (
        (NZ,), (3, NZ), (CHUNKS, NX), (len(PARTS), 2, 7), (len(PARTS), 2), (len(PARTS), 8),
        (CHUNKS, NX), (CHUNKS, NX), (CHUNKS, SLOTS),
    ):
        scratch += [dma(shape), dma(shape)]
    scratch.append(dma((3,)))
    return pl.pallas_call(
        kernel,
        out_shape=jax.ShapeDtypeStruct((OWN, W), BF16),
        in_specs=[pl.BlockSpec(memory_space=pltpu.VMEM)] * 2 + [pl.BlockSpec(memory_space=pl.ANY)] * 3,
        out_specs=pl.BlockSpec(memory_space=pltpu.VMEM),
        scratch_shapes=scratch,
        compiler_params=pltpu.CompilerParams(
            collective_id=0, has_side_effects=True, vmem_limit_bytes=60 << 20
        ),
        name="mlp_input_grad",
    )(inputs, cotangent, up_weight, down_weight, up_bias[None, :])


def solution(mesh):
    return jax.shard_map(
        body,
        mesh=mesh,
        in_specs=(
            P("dp", "tensor"),
            P("dp", "tensor"),
            P("tensor", "dp"),
            P("dp", "tensor"),
            P("dp"),
        ),
        out_specs=P("dp", "tensor"),
        check_vma=False,
    )
```

```python
import functools

import jax
import jax.numpy as jnp
from jax import lax
from jax.experimental import pallas as pl
from jax.experimental.pallas import tpu as pltpu
from jax.sharding import PartitionSpec as P

MESH = pl.DeviceIdType.MESH
BF16, F32 = jnp.bfloat16, jnp.float32

NX, NZ, NC, NY = 4, 8, 2, 8
OWN = 20
W = 384
TILE = 16
WIDE = W + 128
SLAB = 2 * TILE
CHUNKS, SLOTS = 2, 4
BLOCK = SLOTS * OWN

OFFSETS = ((0, 1, 7, 2), (6, 3, 5, 4))
WHERE = {off: (k, j) for k, row in enumerate(OFFSETS) for j, off in enumerate(row)}

PARTS = ((0, 0, 48), (0, 48, 32), (1, 0, 48), (1, 48, 32))

SQRT_2_OVER_PI = 0.7978845608028654
CUBE = 0.044715


def grid_of(rows, columns):
    shape = (rows, columns)
    return lax.broadcasted_iota(jnp.int32, shape, 0), lax.broadcasted_iota(jnp.int32, shape, 1)


def ones_where(mask):
    return jnp.where(mask, 1.0, 0.0).astype(BF16)


def tail_select(group, row, column):
    return (row >= 4 * group) & (row < 4 * group + 4) & (column == TILE + row - 4 * group)


def pack_own(ref):
    i, j = grid_of(TILE, OWN)
    tail = jnp.zeros((TILE, 128), F32)
    for g in range(3):
        tail += dot(ones_where(tail_select(g, i, j)), ref[:, 128 * g : 128 * g + 128])
    return ref[0:TILE, :], tail.astype(BF16)


def unpack_select():
    i, s = grid_of(2 * BLOCK, SLOTS * SLAB)
    kind = (i >= BLOCK).astype(jnp.int32)
    r = i - BLOCK * kind
    slot = sum((r >= OWN * j).astype(jnp.int32) for j in range(1, SLOTS))
    r = r - OWN * slot
    at = SLAB * slot + TILE * kind
    yield ones_where((r < TILE) & (s == at + r))
    for g in range(3):
        yield ones_where((r >= TILE) & (s == at + 4 * g + r - TILE))


def spread_select():
    o, i = grid_of(SLOTS * TILE, BLOCK)
    slot = sum((o >= TILE * j).astype(jnp.int32) for j in range(1, SLOTS))
    r, i = o - TILE * slot, i - OWN * slot
    yield ones_where(i == r)
    for g in range(3):
        yield ones_where(tail_select(g, r, i))


def unpack_out(packed):
    r, s = grid_of(OWN, TILE)
    main = dot(ones_where((r < TILE) & (s == r)), packed[:, :W])
    tails = [dot(ones_where((r >= TILE) & (s == 4 * g + r - TILE)), packed[:, W:]) for g in range(3)]
    return main + jnp.concatenate(tails, axis=1)


def dot(a, b):
    return jnp.dot(a, b, preferred_element_type=F32)


def dot_t(a, b):
    return lax.dot_general(a, b, (((1,), (1,)), ((), ())), preferred_element_type=F32)


def gelu_slope(v):
    u = SQRT_2_OVER_PI * (v + CUBE * (v * v * v))
    t = jnp.tanh(u)
    du = SQRT_2_OVER_PI * (1.0 + (3.0 * CUBE) * (v * v))
    return 0.5 * (1.0 + t) + 0.5 * v * (1.0 - t * t) * du


def kernel(
    x_ref, cot_ref, up_hbm, down_hbm, bias_hbm, out_ref,
    up_ref, down_ref, bias_ref, slab_ref, pack_ref, spread_ref,
    gath, part, ysend, yrecv, zsend, zrecv, hid, prod, csend, crecv, xsend, xrecv, fsend, frecv,
    az_s, az_r, ax_s, ax_r, ac_s, ac_r, y_s, y_r, zh_s, zh_r, h_s, h_r, c_s, c_r, x_s, x_r, f_s, f_r, load_s,
):
    d, t = lax.axis_index("dp"), lax.axis_index("tensor")
    x, z, c = d // (NZ * NC), (d // NC) % NZ, d % NC
    y, zh = t // 2, t % 2
    ring = jnp.where(z % 2 == 0, z // 2, NZ - 1 - z // 2)

    def dev(x=x, z=z, c=c, y=y, zh=zh):
        return ((x * NZ + z) * NC + c, y * 2 + zh)

    def at_ring(off):
        r = (ring + off) % NZ
        return dev(z=jnp.where(r < NZ // 2, 2 * r, 2 * NZ - 1 - 2 * r))

    def at_x(off):
        return dev(x=(x + off) % NX)

    def at_y(off):
        return dev(y=(y + off) % NY)

    sibling, far = dev(c=1 - c), dev(zh=1 - zh)

    sends = []

    def send(src, dst, ssem, rsem, device, keep=True):
        copy = pltpu.make_async_remote_copy(
            src_ref=src, dst_ref=dst, send_sem=ssem, recv_sem=rsem, device_id=device, device_id_type=MESH
        )
        copy.start()
        if keep:
            sends.append(copy)

    def arrived(ref, rsem):
        pltpu.make_async_copy(ref, ref, rsem).wait()

    def left(src, dst, ssem, rsem, device):
        pltpu.make_async_remote_copy(
            src_ref=src, dst_ref=dst, send_sem=ssem, recv_sem=rsem, device_id=device, device_id_type=MESH
        ).wait_send()

    loads = []
    for i, (src, dst) in enumerate(
        ((up_hbm, up_ref), (down_hbm, down_ref), (bias_hbm, bias_ref))
    ):
        loads.append(pltpu.make_async_copy(src, dst, load_s.at[i]))
        loads[-1].start()

    peers = [sibling, far, at_y(1), at_y(-1)]
    peers += [at_x(o) for o in range(1, NX)] + [at_ring(o) for o in range(1, NZ)]
    barrier = pltpu.get_barrier_semaphore()
    for peer in peers:
        pl.semaphore_signal(barrier, inc=1, device_id=peer, device_id_type=MESH)
    for i, ref in enumerate((x_ref, cot_ref)):
        rows = slice(TILE * i, TILE * i + TILE)
        slab_ref[rows, :W], slab_ref[rows, W:] = pack_own(ref)
    gath[0, 0, pl.ds(c, 1), 0:SLAB, :] = slab_ref[...][None]
    pl.semaphore_wait(barrier, len(peers))

    def slot(off, q=0, rows=SLAB, start=0):
        k, j = WHERE[off % NZ]
        return gath.at[k, q % NX, c, pl.ds(SLAB * j + start, rows)]

    def z_own():
        for way in (2, -2, 1, -1):
            at = -way % NZ
            send(slab_ref, slot(at), az_s.at[at], az_r.at[at], at_ring(way))
        x_send(0)

    def z_pass(way):
        off = -2 * way % NZ
        arrived(slot(off), az_r.at[off])
        at = -3 * way % NZ
        send(slot(off), slot(at), az_s.at[at], az_r.at[at], at_ring(way))
        rows, start, i = (TILE, 0, 4) if way == 1 else (TILE, TILE, 0)
        send(slot(off, 0, rows, start), slot(4, 0, rows, start), az_s.at[i], az_r.at[i], at_ring(2 * way))
        x_send(off)

    def z_take(off):
        off %= NZ
        if off == 4:
            arrived(slot(4, 0, TILE, 0), az_r.at[4])
            arrived(slot(4, 0, TILE, TILE), az_r.at[0])
        else:
            arrived(slot(off), az_r.at[off])
        x_send(off)

    def x_send(off):
        for i, way in enumerate((1, -1)):
            src = slab_ref if off == 0 else slot(off)
            send(src, slot(off, -way), ax_s.at[i, off], ax_r.at[i, off], at_x(way))

    def x_take(off):
        off %= NZ
        for i, way in enumerate((1, -1)):
            arrived(slot(off, -way), ax_r.at[i, off])
            if i == WHERE[off][1] % 2:
                send(slot(off, -way), slot(off, 2), ax_s.at[2, off], ax_r.at[2, off], at_x(way))

    def x_last(k):
        for off in OFFSETS[k]:
            arrived(slot(off, 2), ax_r.at[2, off])
        core_send(k, 2)

    def core_send(k, q):
        send(gath.at[k, q, c], gath.at[k, q, c], ac_s.at[k, q], ac_r.at[k, q], sibling)

    def core_wait(k):
        for q in range(NX):
            arrived(gath.at[k, q, 1 - c], ac_r.at[k, q])

    def selects():
        for i, m in enumerate(unpack_select()):
            pack_ref[i] = m
        for i, m in enumerate(spread_select()):
            spread_ref[i] = m

    def partial(k, dist):
        o = (y + dist) % NY
        slabs = gath[k, o // NC, o % NC]
        tails = [dot(pack_ref[1 + g], slabs[:, W:]) for g in range(3)]
        rows = (dot(pack_ref[0], slabs[:, :W]) + jnp.concatenate(tails, axis=1)).astype(BF16)
        part[k, dist % NY, 0] = dot(rows[:BLOCK], up_ref[...])
        part[k, dist % NY, 1] = dot_t(rows[BLOCK:], down_ref[...])

    def rows_of(p):
        k, start, rows = PARTS[p]
        return k, pl.ds(start, rows)

    def y_step(p, m):
        k, rows = rows_of(p)
        dist = 4 - (m + 1) // 2
        for i, way in enumerate((1, -1)):
            which = (m + 1 + i) % 2
            total = part[k, (way * dist) % NY, which, rows, :]
            if m >= 2:
                arrived(yrecv.at[k, i, m - 2, rows], y_r.at[p, i, m - 2])
                total = total + yrecv[k, i, m - 2, rows, :].astype(F32)
            ysend[k, i, m, rows, :] = total.astype(BF16)
            send(ysend.at[k, i, m, rows], yrecv.at[k, i, m, rows], y_s.at[p, i, m], y_r.at[p, i, m], at_y(way))

    def y_last(p):
        k, rows = rows_of(p)
        for which in range(2):
            total = part[k, 0, which, rows, :]
            for i, m in ((0, 5 + which), (1, 6 - which)):
                arrived(yrecv.at[k, i, m, rows], y_r.at[p, i, m])
                total = total + yrecv[k, i, m, rows, :].astype(F32)
            part[k, 0, which, rows, :] = total
            zsend[k, which, rows, :] = total.astype(BF16)
            send(zsend.at[k, which, rows], zrecv.at[k, which, rows], zh_s.at[p, which], zh_r.at[p, which], far)

    def hidden(p):
        k, rows = rows_of(p)
        arrived(zrecv.at[k, 0, rows], zh_r.at[p, 0])
        slope = gelu_slope(part[k, 0, 0, rows, :] + zrecv[k, 0, rows, :].astype(F32) + bias_ref[...][None, :])
        arrived(zrecv.at[k, 1, rows], zh_r.at[p, 1])
        value = ((part[k, 0, 1, rows, :] + zrecv[k, 1, rows, :].astype(F32)) * slope).astype(BF16)
        hid[k, pl.ds(y, 1), rows, :] = value[None]

    def h_block(p, dist, side=None):
        k, start, rows = PARTS[p]
        if side is not None:
            first = 32 if rows == 48 else 16
            start, rows = (start, first) if side == 0 else (start + first, rows - first)
        return hid.at[k, (y + dist + NY) % NY, pl.ds(start, rows)]

    def h_copy(p, dist, way, i, side=None):
        piece = h_block(p, dist, side)
        send(piece, piece, h_s.at[p, i], h_r.at[p, i], at_y(way))

    def h_own(p):
        for i, way in enumerate((2, -2, 1, -1)):
            h_copy(p, 0, way, i)

    def h_pass(p):
        for i, way in enumerate((1, -1)):
            arrived(h_block(p, -2 * way), h_r.at[p, i])
            h_copy(p, -2 * way, way, 4 + i)
            h_copy(p, -2 * way, 2 * way, 6 + i, i)

    def h_near(p):
        for i, way in enumerate((1, -1)):
            arrived(h_block(p, -way), h_r.at[p, 2 + i])

    def h_last(p):
        for i, way in enumerate((1, -1)):
            arrived(h_block(p, -3 * way), h_r.at[p, 4 + i])
            arrived(h_block(p, 4, i), h_r.at[p, 6 + i])

    def pair(dist, own):
        first = y + dist + NY
        o = (first + (first + c + (0 if own else 1)) % 2) % NY
        return o // NC, o

    def product(k, dist):
        q, o = pair(dist, False)
        csend[k, q] = dot_t(hid[k, o], up_ref[...]).astype(BF16)
        send(csend.at[k, q], crecv.at[k, q], c_s.at[k, q], c_r.at[k, q], sibling, False)
        q, o = pair(dist, True)
        prod[k, q] = dot_t(hid[k, o], up_ref[...])

    def over_cores(k, dist):
        q, _ = pair(dist, True)
        arrived(crecv.at[k, q], c_r.at[k, q])
        total = prod[k, q] + crecv[k, q].astype(F32)
        prod[k, q] = total
        xsend[k, q] = total.astype(BF16)

        @pl.when(q != 0)
        def _():
            send(xsend.at[k, q], xrecv.at[k, q], x_s.at[k, q], x_r.at[k, q], at_x(q), False)

    def over_x(k):
        total = prod[k, 0]
        for q in (1, 3, 2):
            arrived(xrecv.at[k, q], x_r.at[k, q])
            total = total + xrecv[k, q].astype(F32)
        total = total.astype(BF16)
        fsend[k, :, :W] = dot(spread_ref[0], total).astype(BF16)
        tails = [dot(spread_ref[1 + g], total[:, 128 * g : 128 * g + 128]) for g in range(3)]
        fsend[k, :, W:] = (tails[0] + tails[1] + tails[2]).astype(BF16)
        for j in range(SLOTS):
            off, rows = OFFSETS[k][j], pl.ds(TILE * j, TILE)
            if off:
                send(fsend.at[k, rows], frecv.at[k, rows], f_s.at[k, j], f_r.at[k, j], at_ring(off))

    def over_z():
        total = fsend[0, 0:TILE, :].astype(F32)
        for k in range(CHUNKS):
            for j in range(SLOTS):
                rows = pl.ds(TILE * j, TILE)
                if OFFSETS[k][j]:
                    arrived(frecv.at[k, rows], f_r.at[k, j])
                    total = total + frecv[k, rows, :].astype(F32)
        out_ref[...] = unpack_out(total.astype(BF16)).astype(BF16)

    z_own()
    selects()
    x_take(0)
    z_pass(1)
    z_pass(-1)
    z_take(1)
    z_take(-1)
    core_send(0, 0)
    x_take(2)
    x_take(-2)
    x_take(1)
    x_take(-1)
    core_send(0, 1)
    core_send(0, 3)
    z_take(3)
    z_take(-3)
    z_take(4)
    core_send(1, 0)
    x_last(0)
    for load in loads:
        load.wait()
    core_wait(0)
    x_take(-3)
    x_take(3)
    x_take(4)
    core_send(1, 1)
    core_send(1, 3)
    partial(0, 4)
    y_step(0, 0)
    partial(0, 3)
    partial(0, -3)
    y_step(0, 1)
    partial(0, 2)
    y_step(1, 0)
    y_step(1, 1)
    partial(0, -2)
    y_step(0, 2)
    partial(0, 0)
    partial(0, 1)
    y_step(0, 3)
    partial(0, -1)
    y_step(1, 2)
    y_step(1, 3)
    x_last(1)
    y_step(0, 4)
    core_wait(1)
    y_step(0, 5)
    partial(1, -3)
    y_step(1, 4)
    y_step(1, 5)
    partial(1, 3)
    y_step(0, 6)
    partial(1, 4)
    y_step(2, 0)
    y_step(2, 1)
    partial(1, -2)
    y_step(1, 6)
    partial(1, 2)
    y_step(3, 0)
    y_step(3, 1)
    y_last(0)
    partial(1, 0)
    y_step(2, 2)
    partial(1, -1)
    y_step(2, 3)
    partial(1, 1)
    y_step(3, 2)
    y_last(1)
    y_step(3, 3)
    y_step(2, 4)
    y_step(2, 5)
    y_step(3, 4)
    y_step(3, 5)
    y_step(2, 6)
    y_step(3, 6)
    y_last(2)
    hidden(0)
    h_own(0)
    y_last(3)
    hidden(1)
    h_own(1)
    h_pass(0)
    h_near(0)
    h_pass(1)
    h_near(1)
    product(0, 0)
    product(0, -2)
    h_last(0)
    hidden(2)
    h_own(2)
    over_cores(0, -2)
    over_cores(0, 0)
    h_last(1)
    product(0, 2)
    product(0, 4)
    over_cores(0, 2)
    hidden(3)
    h_own(3)
    h_pass(2)
    over_cores(0, 4)
    h_near(2)
    h_pass(3)
    h_near(3)
    product(1, -2)
    product(1, 0)
    over_x(0)
    over_cores(1, -2)
    h_last(2)
    over_cores(1, 0)
    h_last(3)
    product(1, 2)
    product(1, 4)
    over_cores(1, 2)
    over_cores(1, 4)
    over_x(1)
    over_z()
    for copy in sends:
        copy.wait_send()
    for k in range(CHUNKS):
        for q in range(NX):
            left(csend.at[k, q], crecv.at[k, q], c_s.at[k, q], c_r.at[k, q], sibling)
            if q:
                left(xsend.at[k, q], xrecv.at[k, q], x_s.at[k, q], x_r.at[k, q], at_x(q))


def body(inputs, cotangent, up_weight, down_weight, up_bias):
    vmem, dma = pltpu.VMEM, pltpu.SemaphoreType.DMA
    scratch = [
        vmem((W, W), BF16),
        vmem((W, W), BF16),
        vmem((W,), F32),
        vmem((SLAB, WIDE), BF16),
        vmem((4, 2 * BLOCK, SLOTS * SLAB), BF16),
        vmem((4, SLOTS * TILE, BLOCK), BF16),
        vmem((CHUNKS, NX, NC, SLOTS * SLAB, WIDE), BF16),
        vmem((CHUNKS, NY, 2, BLOCK, W), F32),
        vmem((CHUNKS, 2, 7, BLOCK, W), BF16),
        vmem((CHUNKS, 2, 7, BLOCK, W), BF16),
        vmem((CHUNKS, 2, BLOCK, W), BF16),
        vmem((CHUNKS, 2, BLOCK, W), BF16),
        vmem((CHUNKS, NY, BLOCK, W), BF16),
        vmem((CHUNKS, NX, BLOCK, W), F32),
        vmem((CHUNKS, NX, BLOCK, W), BF16),
        vmem((CHUNKS, NX, BLOCK, W), BF16),
        vmem((CHUNKS, NX, BLOCK, W), BF16),
        vmem((CHUNKS, NX, BLOCK, W), BF16),
        vmem((CHUNKS, SLOTS * TILE, WIDE), BF16),
        vmem((CHUNKS, SLOTS * TILE, WIDE), BF16),
    ]
    for shape in (
        (NZ,), (3, NZ), (CHUNKS, NX), (len(PARTS), 2, 7), (len(PARTS), 2), (len(PARTS), 8),
        (CHUNKS, NX), (CHUNKS, NX), (CHUNKS, SLOTS),
    ):
        scratch += [dma(shape), dma(shape)]
    scratch.append(dma((3,)))
    return pl.pallas_call(
        kernel,
        out_shape=jax.ShapeDtypeStruct((OWN, W), BF16),
        in_specs=[pl.BlockSpec(memory_space=pltpu.VMEM)] * 2 + [pl.BlockSpec(memory_space=pl.ANY)] * 3,
        out_specs=pl.BlockSpec(memory_space=pltpu.VMEM),
        scratch_shapes=scratch,
        compiler_params=pltpu.CompilerParams(
            collective_id=0, has_side_effects=True, vmem_limit_bytes=60 << 20
        ),
        name="mlp_input_grad",
    )(inputs, cotangent, up_weight, down_weight, up_bias)


def solution(mesh):
    return jax.shard_map(
        body,
        mesh=mesh,
        in_specs=(
            P("dp", "tensor"),
            P("dp", "tensor"),
            P("tensor", "dp"),
            P("dp", "tensor"),
            P("dp"),
        ),
        out_specs=P("dp", "tensor"),
        check_vma=False,
    )
```
